512 devices in a mesh: ctx: 32 (over y_lo, z, core), ch: 16 (over y_hi, x).
Axes of the slice: x: 4, y: 8 (y_hi: 4, y_lo: 2; y = y_hi * 2 + y_lo), z: 8, core: 2. Of those that a mesh axis runs over, the one named last changes fastest.
Arguments:
- query_proj: bfloat16 [4096, 4096], P('ctx', 'ch'), may hold values from -6 to 6
- key_proj: bfloat16 [4096, 4096], P('ctx', 'ch'), may hold values from -6 to 6
- value_proj: bfloat16 [4096, 4096], P('ctx', 'ch'), may hold values from -6 to 6
- cotangent: bfloat16 [4096, 4096], P('ctx', 'ch'), may hold values from -6 to 6
- filter_basis: bfloat16 [4096, 64], P('ctx'), may hold values from -6 to 6
- filter_weight: bfloat16 [64, 4096], P(None, 'ch'), may hold values from -0.125 to 0.125
- decay_rate: float32 [4096], P('ch'), may hold values from 6.1035156e-05 to 0.0014648438
- skip_weight: float32 [4096], P('ch'), may hold values from 0.5 to 1.5
- norm_gain: float32 [4096], P('ch'), may hold values from 0.1 to 1.9
Outputs:
- output: bfloat16 [4096, 4096], P('ctx', 'ch')
- grad_query: bfloat16 [4096, 4096], P('ctx', 'ch')
- grad_key: bfloat16 [4096, 4096], P('ctx', 'ch')
- grad_value: bfloat16 [4096, 4096], P('ctx', 'ch')
- grad_filter: float32 [64, 4096], P('ctx', 'ch')
The draws below stay inside these ranges and needn't reach their ends.
All inputs are finite; a program needn't handle non-finite values.
Results may differ from the reference program's by a relative error of at most 0.0015.
Values sent between devices are 32-bit elements; how exact they have to be, the bound alone decides.
A program may use at most 64 MiB of HBM per device.

```python
import math
import jax
import jax.numpy as jnp
from jax import lax

C = 4096
F = 64
TOKENS = 4096


def with_spikes(result, stream_key, source, target, shards_of, factor):
    def block_of(dim):
        return (jnp.arange(result.shape[dim]) // (result.shape[dim] // shards_of)).reshape((-1,) + (1,) * (result.ndim - 1 - dim))

    one_side = jax.random.permutation(stream_key, shards_of)[block_of(target)]
    far = (block_of(target) + shards_of // 2) % shards_of
    return jnp.where((block_of(source) == one_side) | (block_of(source) == far), factor * result, result)


def level_of(stream_key, extent, pieces, smallest, high):
    factor_of = 1.0
    for axis_at, blocks in pieces:
        heights = jax.random.uniform(jax.random.fold_in(jax.random.fold_in(stream_key, 6), axis_at), (blocks,), jnp.float32, smallest / len(pieces), high / len(pieces))
        factor_of = factor_of * jnp.repeat(jnp.exp(heights), extent[axis_at] // blocks).reshape((-1,) + (1,) * (len(extent) - 1 - axis_at))
    return factor_of


def bell_draw(stream_key, dims, deviation, reach, shards=(), kind=jnp.bfloat16):
    entries = jax.random.normal(stream_key, dims, jnp.float32) * deviation
    if len(shards) > 0:
        entries = level_of(stream_key, dims, shards, -0.22, 0.18) * entries
    return jnp.clip(entries, min=-reach, max=reach).astype(kind)


def noise_with(own_key, dims, spread, limit, split, heavy, kind=jnp.bfloat16):
    result = spread * jax.random.normal(own_key, dims, jnp.float32)
    if split:
        result = result * level_of(own_key, dims, split, -0.22, 0.18)
    return jnp.clip(with_spikes(result, jax.random.fold_in(own_key, 3), *heavy), -limit, limit).astype(kind)


def setup_inputs(seed: int = 0) -> dict:
    streams_of = jax.random.split(jax.random.key(seed), 10)
    return {
        "query_proj": bell_draw(streams_of[0], (TOKENS, C), 1.0, 6.0, ((0, 32), (1, 16))),
        "key_proj": bell_draw(streams_of[1], (TOKENS, C), 1.0, 6.0, ((0, 32), (1, 16))),
        "value_proj": bell_draw(streams_of[2], (TOKENS, C), 1.0, 6.0, ((0, 32), (1, 16))),
        "cotangent": bell_draw(streams_of[3], (TOKENS, C), 1.0, 6.0, ((0, 32), (1, 16))),
        "filter_basis": noise_with(streams_of[4], (TOKENS, F), 1.0, 6.0, ((0, 32),), (0, 1, 32, 2.75)),
        "filter_weight": bell_draw(streams_of[5], (F, C), (32 * F) ** -0.5, 0.125, ((1, 16),)),
        "decay_rate": jnp.clip(jnp.exp(math.log(0.0014648438) - 3.1780538 * jax.random.uniform(streams_of[6], (C,), jnp.float32) ** level_of(streams_of[6], (C,), ((0, 16),), -0.2, 0.2)), 6.103515625e-05, 0.0014648438),
        "skip_weight": jnp.clip(0.5 + 1.0 * jax.random.uniform(streams_of[7], (C,), jnp.float32) ** level_of(streams_of[7], (C,), ((0, 16),), -0.2, 0.2), 0.5, 1.5),
        "norm_gain": jnp.clip(1.0 + 0.18 * jax.random.normal(streams_of[8], (C,), jnp.float32), 0.1, 1.9),
    }


def reference(query_proj, key_proj, value_proj, cotangent, filter_basis, filter_weight, decay_rate, skip_weight, norm_gain):
    position = jnp.arange(TOKENS, dtype=jnp.int32).astype(jnp.float32)
    decay = jnp.exp(-decay_rate[None, :] * position[:, None])
    kernel = jnp.dot(filter_basis, filter_weight, preferred_element_type=jnp.float32) * decay
    queries = query_proj.astype(jnp.float32)
    keys_full = key_proj.astype(jnp.float32)
    values_full = value_proj.astype(jnp.float32)
    gated = keys_full * values_full
    padded = 2 * TOKENS
    gated_spec = jnp.fft.rfft(gated, n=padded, axis=0)
    kernel_spec = jnp.fft.rfft(kernel, n=padded, axis=0)
    conv = jnp.fft.irfft(gated_spec * kernel_spec, n=padded, axis=0)[:TOKENS]
    mixed = conv + skip_weight[None, :] * gated
    signal = queries * mixed
    square_sum = lax.optimization_barrier(jnp.sum(signal * signal, axis=1))
    inv_rms = lax.rsqrt(square_sum / C + 1e-06)
    output = (signal * inv_rms[:, None] * norm_gain[None, :]).astype(jnp.bfloat16)
    scaled = norm_gain[None, :] * cotangent.astype(jnp.float32)
    slope = lax.optimization_barrier(jnp.sum(signal * scaled, axis=1))
    grad_signal = inv_rms[:, None] * scaled - signal * (inv_rms ** 3 * slope / C)[:, None]
    grad_query = (grad_signal * mixed).astype(jnp.bfloat16)
    grad_mixed = grad_signal * queries
    grad_spec = jnp.fft.rfft(grad_mixed, n=padded, axis=0)
    grad_gated = jnp.fft.irfft(jnp.conj(kernel_spec) * grad_spec, n=padded, axis=0)[:TOKENS]
    grad_gated = grad_gated + skip_weight[None, :] * grad_mixed
    grad_key = (grad_gated * values_full).astype(jnp.bfloat16)
    grad_value = (grad_gated * keys_full).astype(jnp.bfloat16)
    grad_kernel = jnp.fft.irfft(jnp.conj(gated_spec) * grad_spec, n=padded, axis=0)[:TOKENS] * decay
    grad_filter = jnp.dot(filter_basis.astype(jnp.float32).T, grad_kernel, precision=lax.Precision.HIGHEST)
    return (output, grad_query, grad_key, grad_value, grad_filter)
```

```python
import functools
import math

import jax
import jax.numpy as jnp
import ml_dtypes
import numpy as np
from jax import lax
from jax.experimental import pallas as pl
from jax.experimental.pallas import tpu as pltpu
from jax.sharding import PartitionSpec as P

MESH = pl.DeviceIdType.MESH
F32 = jnp.float32
BF16 = jnp.bfloat16


def halves(table):
    high = table.astype(np.float32).astype(ml_dtypes.bfloat16)
    low = (table - high.astype(np.float64)).astype(ml_dtypes.bfloat16)
    return high, low


def transform_tables(blocks, rows, group):
    half = 2 * blocks
    odd = 2 * np.arange(blocks) + 1
    angle = math.pi * odd[:, None] * np.arange(blocks)[None, :] / half
    eye = np.eye(group)
    cos_part = np.kron(np.cos(angle), eye)
    sin_part = np.kron(np.sin(angle), eye)
    outer = np.concatenate([cos_part, -sin_part], 0)
    outer_back = np.concatenate([cos_part.T, -sin_part.T], 1) / (blocks * rows)
    index = np.arange(rows)
    inner_angle = 2.0 * math.pi * (index[:, None] * index[None, :] % rows) / rows
    inner_cos, inner_sin = np.cos(inner_angle), -np.sin(inner_angle)
    inner = np.block([[inner_cos, inner_sin], [-inner_sin, inner_cos]])
    turn = np.repeat(math.pi * odd[:, None] * index[None, :] / (half * rows), group, 0)
    turns = np.stack([np.cos(turn), -np.sin(turn)]).astype(np.float32)
    return (*halves(outer), *halves(outer_back), *halves(inner), turns)


def split(x):
    high = x.astype(BF16)
    return high, (x - high.astype(F32)).astype(BF16)


def dot(a, b):
    return jnp.dot(a, b, preferred_element_type=F32)


def dot3(a, b):
    return dot(a[0], b[0]) + dot(a[0], b[1]) + dot(a[1], b[0])


def kernel(
    n_ctx, n_ch,
    q_ref, k_ref, v_ref, ct_ref, basis_ref, weight_ref, rate_ref, skip_ref, gain_ref,
    outer_hi, outer_lo, back_hi, back_lo, inner_hi, inner_lo, turns,
    out_ref, gq_ref, gk_ref, gv_ref, gf_ref,
    send_g, send_k, send_c, send_m, send_x, send_y, send_s, send_f,
    recv_g, recv_k, recv_c, recv_m, recv_x, recv_y, recv_s, recv_f,
    send_sem, recv_sem,
):
    rows, width = q_ref.shape
    group = width // n_ctx
    full_width = width * n_ch
    me = lax.axis_index("ctx")
    my_ch = lax.axis_index("ch")

    barrier = pltpu.get_barrier_semaphore()

    def greet_ctx(d, carry):
        to = lax.rem(me + d, n_ctx)
        pl.semaphore_signal(barrier, inc=1, device_id={"ctx": to}, device_id_type=MESH)
        return carry

    def greet_ch(d, carry):
        to = lax.rem(my_ch + d, n_ch)
        pl.semaphore_signal(barrier, inc=1, device_id={"ch": to}, device_id_type=MESH)
        return carry

    lax.fori_loop(1, n_ctx, greet_ctx, 0)
    lax.fori_loop(1, n_ch, greet_ch, 0)

    def exchange(slot, src, dst):
        def step(d, carry):
            to = lax.rem(me + d, n_ctx)
            pltpu.make_async_remote_copy(
                src_ref=src.at[pl.ds(pl.multiple_of(to * group, group), group)],
                dst_ref=dst.at[pl.ds(pl.multiple_of(me * group, group), group)],
                send_sem=send_sem.at[slot],
                recv_sem=recv_sem.at[slot],
                device_id={"ctx": to},
                device_id_type=MESH,
            ).start()
            return carry

        lax.fori_loop(1, n_ctx, step, 0)
        own = pl.ds(pl.multiple_of(me * group, group), group)
        dst[own] = src[own]

    def all_of(slot, src, dst, extent, axis, count):
        return pltpu.make_async_remote_copy(
            src_ref=src.at[extent],
            dst_ref=dst.at[extent],
            send_sem=send_sem.at[slot],
            recv_sem=recv_sem.at[slot],
            device_id={axis: count},
            device_id_type=MESH,
        )

    others = pl.ds(0, (n_ctx - 1) * group)
    neighbour = lax.rem(me + 1, n_ctx)

    def arrived(slot, src, dst):
        all_of(slot, src, dst, others, "ctx", neighbour).wait_recv()

    def left(slot, src, dst):
        all_of(slot, src, dst, others, "ctx", neighbour).wait_send()

    outer = (outer_hi[...], outer_lo[...])
    back = (back_hi[...], back_lo[...])
    inner = (inner_hi[...], inner_lo[...])
    turn_cos, turn_sin = turns[0], turns[1]

    def turned(real, imag):
        return jnp.concatenate(
            [real * turn_cos - imag * turn_sin, real * turn_sin + imag * turn_cos], 1
        )

    def forward(blocks):
        first = dot3(outer, split(jnp.concatenate(blocks, 1)))
        parts = []
        for at in range(len(blocks)):
            columns = slice(at * rows, (at + 1) * rows)
            parts.append(turned(first[:width, columns], first[width:, columns]))
        spectra = dot3(split(jnp.concatenate(parts, 0)), inner)
        return [
            (spectra[at * width : (at + 1) * width, :rows], spectra[at * width : (at + 1) * width, rows:])
            for at in range(len(blocks))
        ]

    def inverse(conjugates):
        stacked = jnp.concatenate([jnp.concatenate(pair, 1) for pair in conjugates], 0)
        first = dot3(split(stacked), inner)
        columns = []
        for at in range(len(conjugates)):
            part = first[at * width : (at + 1) * width]
            z = turned(part[:, :rows], part[:, rows:])
            columns.append(jnp.concatenate([z[:, :rows], -z[:, rows:]], 0))
        return dot3(back, split(jnp.concatenate(columns, 1)))

    position = (me * rows + lax.broadcasted_iota(jnp.int32, (rows, width), 0)).astype(F32)
    decay = jnp.exp(-rate_ref[...] * position)
    filter_block = dot(basis_ref[...], weight_ref[...]) * decay
    send_k[...] = filter_block.T
    keys = k_ref[...].astype(F32)
    values = v_ref[...].astype(F32)
    gated = (keys * values).T
    send_g[...] = gated

    pl.semaphore_wait(barrier, n_ctx + n_ch - 2)
    exchange(0, send_k, recv_k)
    exchange(1, send_g, recv_g)

    queries = q_ref[...].astype(F32).T
    scaled = (ct_ref[...].astype(F32) * gain_ref[...]).T
    skip = jnp.broadcast_to(skip_ref[...], (rows, width)).T
    gain = gain_ref[...]

    arrived(0, send_k, recv_k)
    arrived(1, send_g, recv_g)
    gated_spec, kernel_spec = forward([recv_g[...], recv_k[...]])

    def product(a, b):
        return a[0] * b[0] - a[1] * b[1], a[0] * b[1] + a[1] * b[0]

    def conj(a):
        return a[0], -a[1]

    send_c[...] = inverse([conj(product(gated_spec, kernel_spec))])
    exchange(2, send_c, recv_c)
    arrived(2, send_c, recv_c)

    mixed = recv_c[...] + skip * gated
    signal = queries * mixed
    send_s[0:1] = jnp.sum(signal * signal, axis=0, keepdims=True)
    send_s[1:2] = jnp.sum(signal * scaled, axis=0, keepdims=True)

    def share(d, carry):
        to = lax.rem(my_ch + d, n_ch)
        pltpu.make_async_remote_copy(
            src_ref=send_s,
            dst_ref=recv_s.at[my_ch],
            send_sem=send_sem.at[3],
            recv_sem=recv_sem.at[3],
            device_id={"ch": to},
            device_id_type=MESH,
        ).start()
        return carry

    lax.fori_loop(1, n_ch, share, 0)
    recv_s[my_ch] = send_s[...]
    sums_wait = pltpu.make_async_remote_copy(
        src_ref=recv_s.at[pl.ds(0, n_ch - 1)],
        dst_ref=recv_s.at[pl.ds(0, n_ch - 1)],
        send_sem=send_sem.at[3],
        recv_sem=recv_sem.at[3],
        device_id={"ch": lax.rem(my_ch + 1, n_ch)},
        device_id_type=MESH,
    )
    sums_wait.wait_recv()
    sums = jnp.sum(recv_s[...], axis=0)
    inv_rms = lax.rsqrt(sums[0:1] / full_width + 1e-06)
    pull = inv_rms * inv_rms * inv_rms * sums[1:2] / full_width
    grad_signal = inv_rms * scaled - signal * pull
    grad_mixed = grad_signal * queries
    send_m[...] = grad_mixed
    exchange(4, send_m, recv_m)

    out_ref[...] = ((signal * inv_rms).T * gain).astype(BF16)
    gq_ref[...] = (grad_signal * mixed).T.astype(BF16)

    arrived(4, send_m, recv_m)
    (grad_spec,) = forward([recv_m[...]])
    both = inverse(
        [product(gated_spec, conj(grad_spec)), product(kernel_spec, conj(grad_spec))]
    )
    send_x[...] = both[:, :rows]
    exchange(5, send_x, recv_x)
    send_y[...] = both[:, rows:]
    exchange(6, send_y, recv_y)

    arrived(5, send_x, recv_x)
    grad_kernel = split(recv_x[...].T * decay)
    basis = basis_ref[...].astype(F32).T.astype(BF16)
    share_f = dot(basis, grad_kernel[0]) + dot(basis, grad_kernel[1])
    each = share_f.shape[0] // n_ctx
    for at in range(n_ctx):
        send_f[at] = share_f[at * each : (at + 1) * each]

    def scatter(d, carry):
        to = lax.rem(me + d, n_ctx)
        pltpu.make_async_remote_copy(
            src_ref=send_f.at[to],
            dst_ref=recv_f.at[me],
            send_sem=send_sem.at[7],
            recv_sem=recv_sem.at[7],
            device_id={"ctx": to},
            device_id_type=MESH,
        ).start()
        return carry

    lax.fori_loop(1, n_ctx, scatter, 0)
    recv_f[me] = send_f[me]

    arrived(6, send_y, recv_y)
    grad_gated = (recv_y[...] + skip * grad_mixed).T
    gk_ref[...] = (grad_gated * values).astype(BF16)
    gv_ref[...] = (grad_gated * keys).astype(BF16)

    filter_wait = all_of(7, send_f, recv_f, pl.ds(0, n_ctx - 1), "ctx", neighbour)
    filter_wait.wait_recv()
    gf_ref[...] = jnp.sum(recv_f[...], axis=0)

    left(0, send_k, recv_k)
    left(1, send_g, recv_g)
    left(2, send_c, recv_c)
    sums_wait.wait_send()
    left(4, send_m, recv_m)
    left(5, send_x, recv_x)
    left(6, send_y, recv_y)
    filter_wait.wait_send()


def solution(mesh):
    n_ctx, n_ch = mesh.shape["ctx"], mesh.shape["ch"]

    def shards(query, key, value, cotangent, basis, weight, rate, skip, gain):
        rows, width = query.shape
        features = basis.shape[1]
        each = features // n_ctx
        tables = transform_tables(n_ctx, rows, width // n_ctx)
        whole = pl.BlockSpec(memory_space=pltpu.VMEM)
        block = (width, rows)
        wide = jax.ShapeDtypeStruct((rows, width), BF16)
        slots = [pltpu.VMEM(block, F32)] * 6
        return pl.pallas_call(
            functools.partial(kernel, n_ctx, n_ch),
            out_shape=(wide, wide, wide, wide, jax.ShapeDtypeStruct((each, width), F32)),
            in_specs=[whole] * (9 + len(tables)),
            out_specs=(whole,) * 5,
            scratch_shapes=[
                *slots,
                pltpu.VMEM((2, rows), F32),
                pltpu.VMEM((n_ctx, each, width), F32),
                *slots,
                pltpu.VMEM((n_ch, 2, rows), F32),
                pltpu.VMEM((n_ctx, each, width), F32),
                pltpu.SemaphoreType.DMA((8,)),
                pltpu.SemaphoreType.DMA((8,)),
            ],
            compiler_params=pltpu.CompilerParams(
                collective_id=0, has_side_effects=True, vmem_limit_bytes=48 * 1024 * 1024
            ),
        )(
            query, key, value, cotangent, basis, weight,
            rate[None, :], skip[None, :], gain[None, :],
            *(jnp.asarray(table) for table in tables),
        )

    return jax.shard_map(
        shards,
        mesh=mesh,
        in_specs=(
            P("ctx", "ch"), P("ctx", "ch"), P("ctx", "ch"), P("ctx", "ch"),
            P("ctx", None), P(None, "ch"), P("ch"), P("ch"), P("ch"),
        ),
        out_specs=(P("ctx", "ch"),) * 5,
        check_vma=False,
    )
```

```python
import functools
import math

import jax
import jax.numpy as jnp
import ml_dtypes
import numpy as np
from jax import lax
from jax.experimental import pallas as pl
from jax.experimental.pallas import tpu as pltpu
from jax.sharding import PartitionSpec as P

MESH = pl.DeviceIdType.MESH
F32 = jnp.float32
BF16 = jnp.bfloat16

N_Y, N_Z, N_CORE = 2, 8, 2
N_CTX = N_Y * N_Z * N_CORE


def halves(table):
    high = table.astype(np.float32).astype(ml_dtypes.bfloat16)
    low = (table - high.astype(np.float64)).astype(ml_dtypes.bfloat16)
    return high, low


def transform_tables(blocks, rows, group):
    half = 2 * blocks
    odd = 2 * np.arange(blocks) + 1
    angle = math.pi * odd[:, None] * np.arange(blocks)[None, :] / half
    eye = np.eye(group)
    cos_part = np.kron(np.cos(angle), eye)
    sin_part = np.kron(np.sin(angle), eye)
    outer = np.concatenate([cos_part, -sin_part], 0)
    outer_back = np.concatenate([cos_part.T, -sin_part.T], 1) / (blocks * rows)
    index = np.arange(rows)
    inner_angle = 2.0 * math.pi * (index[:, None] * index[None, :] % rows) / rows
    inner_cos, inner_sin = np.cos(inner_angle), -np.sin(inner_angle)
    inner = np.block([[inner_cos, inner_sin], [-inner_sin, inner_cos]])
    turn = np.repeat(math.pi * odd[:, None] * index[None, :] / (half * rows), group, 0)
    turns = np.stack([np.cos(turn), -np.sin(turn)]).astype(np.float32)
    return np.stack(halves(outer)), np.stack(halves(outer_back)), np.stack(halves(inner)), turns


def split(x):
    high = x.astype(BF16)
    return high, (x - high.astype(F32)).astype(BF16)


def dot(a, b):
    return jnp.dot(a, b, preferred_element_type=F32)


def dot_nt(a, b):
    return lax.dot_general(a, b, (((1,), (1,)), ((), ())), preferred_element_type=F32)


def dot3(a, b):
    return dot(a[0], b[0]) + dot(a[0], b[1]) + dot(a[1], b[0])


def product(a, b):
    return a[0] * b[0] - a[1] * b[1], a[0] * b[1] + a[1] * b[0]


def conj(a):
    return a[0], -a[1]


def kernel(
    n_ch,
    q_hbm, k_hbm, v_hbm, ct_hbm, basis_hbm, weight_hbm, rate_hbm, skip_hbm, gain_hbm,
    outer_hbm, back_hbm, inner_hbm, turns_hbm,
    out_ref, gq_ref, gk_ref, gv_ref, gf_ref,
    q_ref, k_ref, v_ref, ct_ref, basis_ref, weight_ref, rate_ref, skip_ref, gain_ref,
    outer_ref, back_ref, inner_ref, turns,
    send_k, send_g, send_c, send_m, send_y, send_s, send_f,
    recv_k, recv_g, recv_c, recv_m, recv_y, recv_s, recv_f,
    all_basis, rates,
    load_sem, send_sem, recv_sem,
):
    width, rows = send_k.shape
    features = basis_ref.shape[0]
    each = features // N_CTX
    group = width // N_CTX
    full_width = width * n_ch
    me = lax.axis_index("ctx")
    my_ch = lax.axis_index("ch")
    my_y, my_z, my_core = me // (N_Z * N_CORE), me // N_CORE % N_Z, me % N_CORE
    y_mate = (my_y + 1) % N_Y * N_Z * N_CORE + me % (N_Z * N_CORE)
    core_mate = me - my_core + (my_core + 1) % N_CORE

    barrier = pltpu.get_barrier_semaphore()

    def greet_ctx(d, carry):
        to = lax.rem(me + d, N_CTX)
        pl.semaphore_signal(barrier, inc=1, device_id={"ctx": to}, device_id_type=MESH)
        return carry

    def greet_ch(d, carry):
        to = lax.rem(my_ch + d, n_ch)
        pl.semaphore_signal(barrier, inc=1, device_id={"ch": to}, device_id_type=MESH)
        return carry

    lax.fori_loop(1, N_CTX, greet_ctx, 0)
    lax.fori_loop(1, n_ch, greet_ch, 0)

    sources = (
        k_hbm, v_hbm, basis_hbm, weight_hbm, rate_hbm,
        q_hbm, ct_hbm, skip_hbm, gain_hbm, outer_hbm, back_hbm, inner_hbm, turns_hbm,
    )
    targets = (
        k_ref, v_ref, basis_ref, weight_ref, rate_ref,
        q_ref, ct_ref, skip_ref, gain_ref, outer_ref, back_ref, inner_ref, turns,
    )
    loads = [
        pltpu.make_async_copy(source, target, load_sem.at[at])
        for at, (source, target) in enumerate(zip(sources, targets))
    ]
    for load in loads:
        load.start()

    def peer(d):
        step, corner = d // 4, d % 4
        away = N_Z // 2 + (step + 1) // 2 * (step % 2 * 2 - 1)
        y = (my_y + 1 - corner // 2) % N_Y
        core = (my_core + 1 - corner % 2) % N_CORE
        return (y * N_Z + (my_z + away) % N_Z) * N_CORE + core

    def exchange(slot, src, dst):
        mine = pl.ds(pl.multiple_of(me * group, group), group)

        def step(d, carry):
            to = peer(d)
            pltpu.make_async_remote_copy(
                src_ref=src.at[pl.ds(pl.multiple_of(to * group, group), group)],
                dst_ref=dst.at[mine],
                send_sem=send_sem.at[slot],
                recv_sem=recv_sem.at[slot],
                device_id={"ctx": to},
                device_id_type=MESH,
            ).start()
            return carry

        lax.fori_loop(0, N_CTX - 1, step, 0)
        dst[mine] = src[mine]

    def wait_for(slot, ref, extent, axis, to):
        return pltpu.make_async_remote_copy(
            src_ref=ref.at[extent],
            dst_ref=ref.at[extent],
            send_sem=send_sem.at[slot],
            recv_sem=recv_sem.at[slot],
            device_id={axis: to},
            device_id_type=MESH,
        )

    def blocks_wait(slot, ref):
        return wait_for(slot, ref, pl.ds(0, (N_CTX - 1) * group), "ctx", core_mate)

    def turned(real, imag):
        cos_w, sin_w = turns[0], turns[1]
        return jnp.concatenate([real * cos_w - imag * sin_w, real * sin_w + imag * cos_w], 1)

    def forward(block):
        first = dot3((outer_ref[0], outer_ref[1]), split(block))
        parts = turned(first[:width], first[width:])
        spectrum = dot3(split(parts), (inner_ref[0], inner_ref[1]))
        return spectrum[:, :rows], spectrum[:, rows:]

    def inverse(conjugates):
        stacked = jnp.concatenate([jnp.concatenate(pair, 1) for pair in conjugates], 0)
        first = dot3(split(stacked), (inner_ref[0], inner_ref[1]))
        columns = []
        for at in range(len(conjugates)):
            part = first[at * width : (at + 1) * width]
            z = turned(part[:, :rows], part[:, rows:])
            columns.append(jnp.concatenate([z[:, :rows], -z[:, rows:]], 0))
        return dot3((back_ref[0], back_ref[1]), split(jnp.concatenate(columns, 1)))

    for load in loads[:5]:
        load.wait()
    rate = jnp.broadcast_to(rate_ref[...], (rows, width)).T
    rates[...] = rate
    lane = lax.broadcasted_iota(jnp.int32, (width, rows), 1)
    decay = jnp.exp(-rate * (me * rows + lane).astype(F32))
    weight = weight_ref[...].astype(F32).T.astype(BF16)
    send_k[...] = dot(weight, basis_ref[...]) * decay
    keys = k_ref[...].astype(F32)
    values = v_ref[...].astype(F32)
    gated = (keys * values).T
    send_g[...] = gated
    all_basis[me] = basis_ref[...].astype(F32)

    pl.semaphore_wait(barrier, N_CTX + n_ch - 2)
    exchange(0, send_k, recv_k)
    exchange(1, send_g, recv_g)

    def spread(d, carry):
        away = N_Z // 2 + (d + 1) // 2 * (d % 2 * 2 - 1)
        to = me - my_z * N_CORE + (my_z + away) % N_Z * N_CORE
        pltpu.make_async_remote_copy(
            src_ref=all_basis.at[me],
            dst_ref=all_basis.at[me],
            send_sem=send_sem.at[4],
            recv_sem=recv_sem.at[4],
            device_id={"ctx": to},
            device_id_type=MESH,
        ).start()
        return carry

    lax.fori_loop(0, N_Z - 1, spread, 0)

    for load in loads[5:]:
        load.wait()
    queries = q_ref[...].astype(F32).T
    scaled = (ct_ref[...].astype(F32) * gain_ref[...]).T
    skip = jnp.broadcast_to(skip_ref[...], (rows, width)).T
    gain = gain_ref[...]

    blocks_wait(0, recv_k).wait_recv()
    kernel_spec = forward(recv_k[...])
    blocks_wait(1, recv_g).wait_recv()
    gated_spec = forward(recv_g[...])
    send_c[...] = inverse([conj(product(gated_spec, kernel_spec))])
    exchange(2, send_c, recv_c)

    own_rate = rates[pl.ds(pl.multiple_of(me * group, group), group)]
    row = lax.broadcasted_iota(jnp.int32, (width, rows), 0)
    own_decay = jnp.exp(
        -jnp.concatenate([own_rate] * N_CTX, 0) * (row // group * rows + lane).astype(F32)
    )

    blocks_wait(2, recv_c).wait_recv()
    mixed = recv_c[...] + skip * gated
    signal = queries * mixed
    send_s[0:1] = jnp.sum(signal * signal, axis=0, keepdims=True)
    send_s[1:2] = jnp.sum(signal * scaled, axis=0, keepdims=True)

    def share(d, carry):
        to = lax.rem(my_ch + d, n_ch)
        pltpu.make_async_remote_copy(
            src_ref=send_s,
            dst_ref=recv_s.at[my_ch],
            send_sem=send_sem.at[3],
            recv_sem=recv_sem.at[3],
            device_id={"ch": to},
            device_id_type=MESH,
        ).start()
        return carry

    lax.fori_loop(1, n_ch, share, 0)
    recv_s[my_ch] = send_s[...]

    wait_for(4, all_basis, pl.ds(0, N_Z - 1), "ctx", core_mate).wait_recv()
    for z in range(N_Z):
        slot = my_y * N_Z * N_CORE + z * N_CORE + my_core
        pltpu.make_async_remote_copy(
            src_ref=all_basis.at[slot],
            dst_ref=all_basis.at[slot],
            send_sem=send_sem.at[8],
            recv_sem=recv_sem.at[8],
            device_id={"ctx": y_mate},
            device_id_type=MESH,
        ).start()

    sums_wait = wait_for(3, recv_s, pl.ds(0, n_ch - 1), "ch", lax.rem(my_ch + 1, n_ch))
    sums_wait.wait_recv()
    sums = jnp.sum(recv_s[...], axis=0)
    inv_rms = lax.rsqrt(sums[0:1] / full_width + 1e-06)
    pull = inv_rms * inv_rms * inv_rms * sums[1:2] / full_width
    grad_signal = inv_rms * scaled - signal * pull
    grad_mixed = grad_signal * queries
    send_m[...] = grad_mixed
    exchange(5, send_m, recv_m)

    out_ref[...] = ((signal * inv_rms).T * gain).astype(BF16)
    gq_ref[...] = (grad_signal * mixed).T.astype(BF16)

    wait_for(8, all_basis, pl.ds(0, N_Z), "ctx", y_mate).wait_recv()
    for at in range(N_Y * N_Z):
        slot = at * N_CORE + my_core
        pltpu.make_async_remote_copy(
            src_ref=all_basis.at[slot],
            dst_ref=all_basis.at[slot],
            send_sem=send_sem.at[9],
            recv_sem=recv_sem.at[9],
            device_id={"ctx": core_mate},
            device_id_type=MESH,
        ).start()

    blocks_wait(5, recv_m).wait_recv()
    grad_spec = conj(forward(recv_m[...]))
    both = inverse([product(kernel_spec, grad_spec), product(gated_spec, grad_spec)])
    send_y[...] = both[:, :rows]
    exchange(6, send_y, recv_y)

    wait_for(9, all_basis, pl.ds(0, N_Y * N_Z), "ctx", core_mate).wait_recv()
    high, low = split(both[:, rows:] * own_decay)
    total = jnp.zeros((features, 2 * group), F32)
    for at in range(N_CTX):
        take = slice(at * group, (at + 1) * group)
        pair = jnp.concatenate([high[take].astype(F32), low[take].astype(F32)], 0).astype(BF16)
        total += dot_nt(all_basis[at].astype(BF16), pair)
    total = total[:, :group] + total[:, group:]
    own_filter = jnp.concatenate([total, jnp.zeros((features, rows - group), F32)], 1)
    own_filter = pltpu.roll(own_filter, me * group % rows, 1)
    for at in range(N_CTX):
        send_f[at] = own_filter[at * each : (at + 1) * each]

    def scatter(d, carry):
        to = peer(d)
        pltpu.make_async_remote_copy(
            src_ref=send_f.at[to],
            dst_ref=recv_f.at[me],
            send_sem=send_sem.at[7],
            recv_sem=recv_sem.at[7],
            device_id={"ctx": to},
            device_id_type=MESH,
        ).start()
        return carry

    lax.fori_loop(0, N_CTX - 1, scatter, 0)
    recv_f[me] = send_f[me]

    blocks_wait(6, recv_y).wait_recv()
    grad_gated = (recv_y[...] + skip * grad_mixed).T
    gk_ref[...] = (grad_gated * values).astype(BF16)
    gv_ref[...] = (grad_gated * keys).astype(BF16)

    filter_wait = wait_for(7, recv_f, pl.ds(0, N_CTX - 1), "ctx", core_mate)
    filter_wait.wait_recv()
    per = rows // group
    for at in range(width // rows):
        gf_ref[:, at * rows : (at + 1) * rows] = jnp.sum(recv_f[at * per : (at + 1) * per], axis=0)

    blocks_wait(0, send_k).wait_send()
    blocks_wait(1, send_g).wait_send()
    blocks_wait(2, send_c).wait_send()
    blocks_wait(5, send_m).wait_send()
    blocks_wait(6, send_y).wait_send()
    sums_wait.wait_send()
    filter_wait.wait_send()
    wait_for(4, all_basis, pl.ds(0, N_Z - 1), "ctx", core_mate).wait_send()
    wait_for(8, all_basis, pl.ds(0, N_Z), "ctx", y_mate).wait_send()
    wait_for(9, all_basis, pl.ds(0, N_Y * N_Z), "ctx", core_mate).wait_send()


def store(*refs):
    count = len(refs) // 2
    copies = [
        pltpu.make_async_copy(refs[at], refs[count + at], refs[-1].at[at]) for at in range(count)
    ]
    for copy in copies:
        copy.start()
    for copy in copies:
        copy.wait()


def solution(mesh):
    n_ctx, n_ch = mesh.shape["ctx"], mesh.shape["ch"]
    assert n_ctx == N_CTX

    def shards(query, key, value, cotangent, basis, weight, rate, skip, gain):
        rows, width = query.shape
        features = basis.shape[1]
        each = features // n_ctx
        tables = transform_tables(n_ctx, rows, width // n_ctx)
        operands = (
            query, key, value, cotangent, basis.T, weight,
            rate[None, :], skip[None, :], gain[None, :],
            *(jnp.asarray(table) for table in tables),
        )
        inside = pl.BlockSpec(memory_space=pltpu.VMEM)
        outside = pl.BlockSpec(memory_space=pltpu.HBM)
        wide = jax.ShapeDtypeStruct((rows, width), BF16)
        results = (wide, wide, wide, wide, jax.ShapeDtypeStruct((each, width), F32))
        slots = [pltpu.VMEM((width, rows), F32)] * 5
        last = [pltpu.VMEM((n_ctx, each, rows), F32)]
        computed = pl.pallas_call(
            functools.partial(kernel, n_ch),
            out_shape=results,
            in_specs=[outside] * len(operands),
            out_specs=(inside,) * 5,
            scratch_shapes=[
                *(pltpu.VMEM(operand.shape, operand.dtype) for operand in operands),
                *slots,
                pltpu.VMEM((2, rows), F32),
                *last,
                *slots,
                pltpu.VMEM((n_ch, 2, rows), F32),
                *last,
                pltpu.VMEM((n_ctx, features, rows), F32),
                pltpu.VMEM((width, rows), F32),
                pltpu.SemaphoreType.DMA((len(operands),)),
                pltpu.SemaphoreType.DMA((10,)),
                pltpu.SemaphoreType.DMA((10,)),
            ],
            compiler_params=pltpu.CompilerParams(
                collective_id=0, has_side_effects=True, vmem_limit_bytes=60 * 1024 * 1024
            ),
        )(*operands)
        return pl.pallas_call(
            store,
            out_shape=results,
            in_specs=[inside] * 5,
            out_specs=(outside,) * 5,
            scratch_shapes=[pltpu.SemaphoreType.DMA((5,))],
        )(*computed)

    return jax.shard_map(
        shards,
        mesh=mesh,
        in_specs=(
            P("ctx", "ch"), P("ctx", "ch"), P("ctx", "ch"), P("ctx", "ch"),
            P("ctx", None), P(None, "ch"), P("ch"), P("ch"), P("ch"),
        ),
        out_specs=(P("ctx", "ch"),) * 5,
        check_vma=False,
    )
```

```python
import functools
import math

import jax
import jax.numpy as jnp
import ml_dtypes
import numpy as np
from jax import lax
from jax.experimental import pallas as pl
from jax.experimental.pallas import tpu as pltpu
from jax.sharding import PartitionSpec as P

MESH = pl.DeviceIdType.MESH
F32 = jnp.float32
BF16 = jnp.bfloat16

N_Y, N_Z, N_CORE = 2, 8, 2
N_CTX = N_Y * N_Z * N_CORE


def halves(table):
    high = table.astype(np.float32).astype(ml_dtypes.bfloat16)
    low = (table - high.astype(np.float64)).astype(ml_dtypes.bfloat16)
    return high, low


def transform_tables(blocks, rows, group):
    half = 2 * blocks
    odd = 2 * np.arange(blocks) + 1
    angle = math.pi * odd[:, None] * np.arange(blocks)[None, :] / half
    eye = np.eye(group)
    cos_part = np.kron(np.cos(angle), eye)
    sin_part = np.kron(np.sin(angle), eye)
    outer = np.concatenate([cos_part, -sin_part], 0)
    outer_back = np.concatenate([cos_part.T, -sin_part.T], 1) / (blocks * rows)
    index = np.arange(rows)
    inner_angle = 2.0 * math.pi * (index[:, None] * index[None, :] % rows) / rows
    inner_cos, inner_sin = np.cos(inner_angle), -np.sin(inner_angle)
    inner = np.block([[inner_cos, inner_sin], [-inner_sin, inner_cos]])
    turn = np.repeat(math.pi * odd[:, None] * index[None, :] / (half * rows), group, 0)
    turns = np.stack([np.cos(turn), -np.sin(turn)]).astype(np.float32)
    return np.stack(halves(outer)), np.stack(halves(outer_back)), np.stack(halves(inner)), turns


def split(x):
    high = x.astype(BF16)
    return high, (x - high.astype(F32)).astype(BF16)


def dot(a, b):
    return jnp.dot(a, b, preferred_element_type=F32)


def dot_nt(a, b):
    return lax.dot_general(a, b, (((1,), (1,)), ((), ())), preferred_element_type=F32)


def dot3(a, b):
    return dot(a[0], b[0]) + dot(a[0], b[1]) + dot(a[1], b[0])


def dot3_wide(a, b):
    columns = b[0].shape[1]
    both = dot(a[0], jnp.concatenate(b, 1))
    return both[:, :columns] + both[:, columns:] + dot(a[1], b[0])


def product(a, b):
    return a[0] * b[0] - a[1] * b[1], a[0] * b[1] + a[1] * b[0]


def conj(a):
    return a[0], -a[1]


def kernel(
    n_ch,
    q_hbm, k_hbm, v_hbm, ct_hbm, basis_hbm, weight_hbm, rate_hbm, skip_hbm, gain_hbm,
    outer_hbm, back_hbm, inner_hbm, turns_hbm,
    out_ref, gq_ref, gk_ref, gv_ref, gf_ref,
    q_ref, k_ref, v_ref, ct_ref, basis_ref, weight_ref, rate_ref, skip_ref, gain_ref,
    outer_ref, back_ref, inner_ref, turns,
    send_k, send_g, send_c, send_m, send_y, send_s, send_f,
    recv_k, recv_g, recv_c, recv_m, recv_y, recv_s, recv_f,
    all_basis, rates, wide_basis, own_grad,
    load_sem, send_sem, recv_sem,
):
    width, rows = send_k.shape
    features = basis_ref.shape[0]
    each = features // N_CTX
    group = width // N_CTX
    full_width = width * n_ch
    me = lax.axis_index("ctx")
    my_ch = lax.axis_index("ch")
    my_y, my_z, my_core = me // (N_Z * N_CORE), me // N_CORE % N_Z, me % N_CORE
    y_mate = (my_y + 1) % N_Y * N_Z * N_CORE + me % (N_Z * N_CORE)
    core_mate = me - my_core + (my_core + 1) % N_CORE

    peers = []
    for dy in (1, 0):
        for dc in (1, 0):
            corner = lax.rem(my_y + dy, N_Y) * (N_Z * N_CORE) + lax.rem(my_core + dc, N_CORE)
            for dz in (4, 3, 5, 2, 6, 1, 7, 0):
                if (dy, dz, dc) != (0, 0, 0):
                    peers.append(corner + lax.rem(my_z + dz, N_Z) * N_CORE)
    half = N_CTX // 2
    other_y = lax.rem(my_y + 1, N_Y)
    ch_peers = [lax.rem(my_ch + d, n_ch) for d in range(1, n_ch)]

    barrier = pltpu.get_barrier_semaphore()

    for to in peers:
        pl.semaphore_signal(barrier, inc=1, device_id={"ctx": to}, device_id_type=MESH)
    for to in ch_peers:
        pl.semaphore_signal(barrier, inc=1, device_id={"ch": to}, device_id_type=MESH)

    sources = (
        k_hbm, v_hbm, basis_hbm, weight_hbm, rate_hbm,
        q_hbm, ct_hbm, skip_hbm, gain_hbm, outer_hbm, back_hbm, inner_hbm, turns_hbm,
    )
    targets = (
        k_ref, v_ref, basis_ref, weight_ref, rate_ref,
        q_ref, ct_ref, skip_ref, gain_ref, outer_ref, back_ref, inner_ref, turns,
    )
    loads = [
        pltpu.make_async_copy(source, target, load_sem.at[at])
        for at, (source, target) in enumerate(zip(sources, targets))
    ]
    for load in loads:
        load.start()

    def exchange(slot, src, dst, to_peers):
        mine = pl.ds(pl.multiple_of(me * group, group), group)
        for to in to_peers:
            pltpu.make_async_remote_copy(
                src_ref=src.at[pl.ds(pl.multiple_of(to * group, group), group)],
                dst_ref=dst.at[mine],
                send_sem=send_sem.at[slot],
                recv_sem=recv_sem.at[slot],
                device_id={"ctx": to},
                device_id_type=MESH,
            ).start()

    def planes_in_order(y, act):
        for z in range(N_Z):
            for core in (lax.rem(my_core + 1, N_CORE), my_core):
                to = (y * N_Z + z) * N_CORE + core

                @pl.when(to != me)
                def _():
                    act(to)

    def give_back(slot, src, dst, to):
        exchange(slot, src, dst, [to])

    def keep_own(src, dst):
        mine = pl.ds(pl.multiple_of(me * group, group), group)
        dst[mine] = src[mine]

    def wait_for(slot, ref, extent, axis, to):
        return pltpu.make_async_remote_copy(
            src_ref=ref.at[extent],
            dst_ref=ref.at[extent],
            send_sem=send_sem.at[slot],
            recv_sem=recv_sem.at[slot],
            device_id={axis: to},
            device_id_type=MESH,
        )

    def blocks_wait(slot, ref):
        return wait_for(slot, ref, pl.ds(0, (N_CTX - 1) * group), "ctx", core_mate)

    def turned(real, imag):
        cos_w, sin_w = turns[0], turns[1]
        return jnp.concatenate([real * cos_w - imag * sin_w, real * sin_w + imag * cos_w], 1)

    def forward(block):
        first = dot3_wide((outer_ref[0], outer_ref[1]), split(block))
        parts = turned(first[:width], first[width:])
        spectrum = dot3(split(parts), (inner_ref[0], inner_ref[1]))
        return spectrum[:, :rows], spectrum[:, rows:]

    def inverse(conjugates):
        stacked = jnp.concatenate([jnp.concatenate(pair, 1) for pair in conjugates], 0)
        first = dot3(split(stacked), (inner_ref[0], inner_ref[1]))
        columns = []
        for at in range(len(conjugates)):
            part = first[at * width : (at + 1) * width]
            z = turned(part[:, :rows], part[:, rows:])
            columns.append(jnp.concatenate([z[:, :rows], -z[:, rows:]], 0))
        return split(jnp.concatenate(columns, 1))

    side = width // N_Y

    def blocks_of(y, columns, multiply):
        take = pl.ds(pl.multiple_of(y * side, side), side)
        return take, multiply((back_ref[0, take], back_ref[1, take]), columns)

    for load in loads[:5]:
        load.wait()
    rate = jnp.broadcast_to(rate_ref[...], (rows, width)).T
    rates[...] = rate
    lane = lax.broadcasted_iota(jnp.int32, (width, rows), 1)
    decay = jnp.exp(-rate * (me * rows + lane).astype(F32))
    weight = weight_ref[...].astype(F32).T.astype(BF16)
    send_k[...] = dot(weight, basis_ref[...]) * decay
    keys = k_ref[...].astype(F32)
    values = v_ref[...].astype(F32)
    gated = (keys * values).T
    send_g[...] = gated
    all_basis[me] = basis_ref[...].astype(F32)

    pl.semaphore_wait(barrier, N_CTX + n_ch - 2)
    exchange(0, send_k, recv_k, peers)
    exchange(1, send_g, recv_g, peers)
    keep_own(send_k, recv_k)
    keep_own(send_g, recv_g)

    def pass_on(slot, origin, away):
        at = me + (lax.rem(my_z + origin, N_Z) - my_z) * N_CORE
        to = me + (lax.rem(my_z + away, N_Z) - my_z) * N_CORE
        pltpu.make_async_remote_copy(
            src_ref=all_basis.at[at],
            dst_ref=all_basis.at[at],
            send_sem=send_sem.at[slot],
            recv_sem=recv_sem.at[slot],
            device_id={"ctx": to},
            device_id_type=MESH,
        ).start()

    for away in (2, N_Z - 2, 1, N_Z - 1):
        pass_on(4, 0, away)

    for load in loads[5:]:
        load.wait()
    queries = q_ref[...].astype(F32).T
    scaled = (ct_ref[...].astype(F32) * gain_ref[...]).T
    skip = jnp.broadcast_to(skip_ref[...], (rows, width)).T
    gain = gain_ref[...]

    blocks_wait(0, recv_k).wait_recv()
    kernel_spec = forward(recv_k[...])
    blocks_wait(1, recv_g).wait_recv()
    gated_spec = forward(recv_g[...])
    columns = inverse([conj(product(gated_spec, kernel_spec))])
    for y, some in ((other_y, peers[:half]), (my_y, peers[half:])):
        take, blocks = blocks_of(y, columns, dot3_wide)
        send_c[take] = blocks
        exchange(2, send_c, recv_c, some)
    keep_own(send_c, recv_c)

    wait_for(4, all_basis, pl.ds(0, 4), "ctx", core_mate).wait_recv()
    pass_on(10, N_Z - 2, 2)
    pass_on(10, N_Z - 2, 1)
    pass_on(10, 2, N_Z - 1)

    own_rate = rates[pl.ds(pl.multiple_of(me * group, group), group)]
    row = lax.broadcasted_iota(jnp.int32, (width, rows), 0)
    own_decay = jnp.exp(
        -jnp.concatenate([own_rate] * N_CTX, 0) * (row // group * rows + lane).astype(F32)
    )

    blocks_wait(2, recv_c).wait_recv()
    mixed = recv_c[...] + skip * gated
    signal = queries * mixed
    send_s[0:1] = jnp.sum(signal * signal, axis=0, keepdims=True)
    send_s[1:2] = jnp.sum(signal * scaled, axis=0, keepdims=True)

    for to in ch_peers:
        pltpu.make_async_remote_copy(
            src_ref=send_s,
            dst_ref=recv_s.at[my_ch],
            send_sem=send_sem.at[3],
            recv_sem=recv_sem.at[3],
            device_id={"ch": to},
            device_id_type=MESH,
        ).start()

    recv_s[my_ch] = send_s[...]

    wait_for(10, all_basis, pl.ds(0, 3), "ctx", core_mate).wait_recv()
    for z in range(N_Z):
        slot = my_y * N_Z * N_CORE + z * N_CORE + my_core
        pltpu.make_async_remote_copy(
            src_ref=all_basis.at[slot],
            dst_ref=all_basis.at[slot],
            send_sem=send_sem.at[8],
            recv_sem=recv_sem.at[8],
            device_id={"ctx": y_mate},
            device_id_type=MESH,
        ).start()

    sums_wait = wait_for(3, recv_s, pl.ds(0, n_ch - 1), "ch", lax.rem(my_ch + 1, n_ch))
    sums_wait.wait_recv()
    sums = jnp.sum(recv_s[...], axis=0)
    inv_rms = lax.rsqrt(sums[0:1] / full_width + 1e-06)
    pull = inv_rms * inv_rms * inv_rms * sums[1:2] / full_width
    grad_signal = inv_rms * scaled - signal * pull
    grad_mixed = grad_signal * queries
    send_m[...] = grad_mixed
    exchange(5, send_m, recv_m, peers)
    keep_own(send_m, recv_m)

    out_ref[...] = ((signal * inv_rms).T * gain).astype(BF16)
    gq_ref[...] = (grad_signal * mixed).T.astype(BF16)

    wait_for(8, all_basis, pl.ds(0, N_Z), "ctx", y_mate).wait_recv()
    for at in range(N_Y * N_Z):
        slot = at * N_CORE + my_core
        pltpu.make_async_remote_copy(
            src_ref=all_basis.at[slot],
            dst_ref=all_basis.at[slot],
            send_sem=send_sem.at[9],
            recv_sem=recv_sem.at[9],
            device_id={"ctx": core_mate},
            device_id_type=MESH,
        ).start()

    wait_for(9, all_basis, pl.ds(0, N_Y * N_Z), "ctx", core_mate).wait_recv()
    for at in range(N_CTX):
        wide_basis[:, at * rows : (at + 1) * rows] = all_basis[at].astype(BF16)

    blocks_wait(5, recv_m).wait_recv()
    grad_spec = conj(forward(recv_m[...]))
    columns = inverse([product(kernel_spec, grad_spec), product(gated_spec, grad_spec)])
    for y in (other_y, my_y):
        take, blocks = blocks_of(y, columns, dot3)
        send_y[take] = blocks[:, :rows]
        planes_in_order(y, functools.partial(give_back, 6, send_y, recv_y))
        own_grad[take] = blocks[:, rows:]
    keep_own(send_y, recv_y)

    high, low = (part.astype(F32) for part in split(own_grad[...] * own_decay))
    pairs = [
        jnp.concatenate([part[at * group : (at + 1) * group] for part in (high, low)], 0)
        for at in range(N_CTX)
    ]
    total = dot_nt(wide_basis[...], jnp.concatenate(pairs, 1).astype(BF16))
    total = total[:, :group] + total[:, group:]
    own_filter = jnp.concatenate([total, jnp.zeros((features, rows - group), F32)], 1)
    own_filter = pltpu.roll(own_filter, me * group % rows, 1)
    for at in range(N_CTX):
        send_f[at] = own_filter[at * each : (at + 1) * each]

    def give_filter(to):
        pltpu.make_async_remote_copy(
            src_ref=send_f.at[to],
            dst_ref=recv_f.at[me],
            send_sem=send_sem.at[7],
            recv_sem=recv_sem.at[7],
            device_id={"ctx": to},
            device_id_type=MESH,
        ).start()

    for y in (other_y, my_y):
        planes_in_order(y, give_filter)
    recv_f[me] = send_f[me]

    blocks_wait(6, recv_y).wait_recv()
    grad_gated = (recv_y[...] + skip * grad_mixed).T
    gk_ref[...] = (grad_gated * values).astype(BF16)
    gv_ref[...] = (grad_gated * keys).astype(BF16)

    filter_wait = wait_for(7, recv_f, pl.ds(0, N_CTX - 1), "ctx", core_mate)
    filter_wait.wait_recv()
    per = rows // group
    for at in range(width // rows):
        gf_ref[:, at * rows : (at + 1) * rows] = jnp.sum(recv_f[at * per : (at + 1) * per], axis=0)

    blocks_wait(0, send_k).wait_send()
    blocks_wait(1, send_g).wait_send()
    blocks_wait(2, send_c).wait_send()
    blocks_wait(5, send_m).wait_send()
    blocks_wait(6, send_y).wait_send()
    sums_wait.wait_send()
    filter_wait.wait_send()
    wait_for(4, all_basis, pl.ds(0, 4), "ctx", core_mate).wait_send()
    wait_for(10, all_basis, pl.ds(0, 3), "ctx", core_mate).wait_send()
    wait_for(8, all_basis, pl.ds(0, N_Z), "ctx", y_mate).wait_send()
    wait_for(9, all_basis, pl.ds(0, N_Y * N_Z), "ctx", core_mate).wait_send()


def store(*refs):
    count = len(refs) // 2
    copies = [
        pltpu.make_async_copy(refs[at], refs[count + at], refs[-1].at[at]) for at in range(count)
    ]
    for copy in copies:
        copy.start()
    for copy in copies:
        copy.wait()


def solution(mesh):
    n_ctx, n_ch = mesh.shape["ctx"], mesh.shape["ch"]
    assert n_ctx == N_CTX

    def shards(query, key, value, cotangent, basis, weight, rate, skip, gain):
        rows, width = query.shape
        features = basis.shape[1]
        each = features // n_ctx
        tables = transform_tables(n_ctx, rows, width // n_ctx)
        operands = (
            query, key, value, cotangent, basis.T, weight,
            rate[None, :], skip[None, :], gain[None, :],
            *(jnp.asarray(table) for table in tables),
        )
        inside = pl.BlockSpec(memory_space=pltpu.VMEM)
        outside = pl.BlockSpec(memory_space=pltpu.HBM)
        wide = jax.ShapeDtypeStruct((rows, width), BF16)
        results = (wide, wide, wide, wide, jax.ShapeDtypeStruct((each, width), F32))
        slots = [pltpu.VMEM((width, rows), F32)] * 5
        last = [pltpu.VMEM((n_ctx, each, rows), F32)]
        computed = pl.pallas_call(
            functools.partial(kernel, n_ch),
            out_shape=results,
            in_specs=[outside] * len(operands),
            out_specs=(inside,) * 5,
            scratch_shapes=[
                *(pltpu.VMEM(operand.shape, operand.dtype) for operand in operands),
                *slots,
                pltpu.VMEM((2, rows), F32),
                *last,
                *slots,
                pltpu.VMEM((n_ch, 2, rows), F32),
                *last,
                pltpu.VMEM((n_ctx, features, rows), F32),
                pltpu.VMEM((width, rows), F32),
                pltpu.VMEM((features, n_ctx * rows), BF16),
                pltpu.VMEM((width, rows), F32),
                pltpu.SemaphoreType.DMA((len(operands),)),
                pltpu.SemaphoreType.DMA((11,)),
                pltpu.SemaphoreType.DMA((11,)),
            ],
            compiler_params=pltpu.CompilerParams(
                collective_id=0, has_side_effects=True, vmem_limit_bytes=60 * 1024 * 1024
            ),
        )(*operands)
        return pl.pallas_call(
            store,
            out_shape=results,
            in_specs=[inside] * 5,
            out_specs=(outside,) * 5,
            scratch_shapes=[pltpu.SemaphoreType.DMA((5,))],
        )(*computed)

    return jax.shard_map(
        shards,
        mesh=mesh,
        in_specs=(
            P("ctx", "ch"), P("ctx", "ch"), P("ctx", "ch"), P("ctx", "ch"),
            P("ctx", None), P(None, "ch"), P("ch"), P("ch"), P("ch"),
        ),
        out_specs=(P("ctx", "ch"),) * 5,
        check_vma=False,
    )
```

```python
import functools
import math

import jax
import jax.numpy as jnp
import ml_dtypes
import numpy as np
from jax import lax
from jax.experimental import pallas as pl
from jax.experimental.pallas import tpu as pltpu
from jax.sharding import PartitionSpec as P

MESH = pl.DeviceIdType.MESH
F32 = jnp.float32
BF16 = jnp.bfloat16

N_Y, N_Z, N_CORE = 2, 8, 2
N_CTX = N_Y * N_Z * N_CORE
N_CH_Y, N_CH_X = 4, 4


def halves(table):
    high = table.astype(np.float32).astype(ml_dtypes.bfloat16)
    low = (table - high.astype(np.float64)).astype(ml_dtypes.bfloat16)
    return high, low


def transform_tables(blocks, rows, group):
    half = 2 * blocks
    odd = 2 * np.arange(blocks) + 1
    angle = math.pi * odd[:, None] * np.arange(blocks)[None, :] / half
    eye = np.eye(group)
    cos_part = np.kron(np.cos(angle), eye)
    sin_part = np.kron(np.sin(angle), eye)
    outer = np.concatenate([cos_part, -sin_part], 0)
    outer_back = np.concatenate([cos_part.T, -sin_part.T], 1) / (blocks * rows)
    index = np.arange(rows)
    inner_angle = 2.0 * math.pi * (index[:, None] * index[None, :] % rows) / rows
    inner_cos, inner_sin = np.cos(inner_angle), -np.sin(inner_angle)
    inner = np.block([[inner_cos, inner_sin], [-inner_sin, inner_cos]])
    turn = np.repeat(math.pi * odd[:, None] * index[None, :] / (half * rows), group, 0)
    turns = np.stack([np.cos(turn), -np.sin(turn)]).astype(np.float32)
    return np.stack(halves(outer)), np.stack(halves(outer_back)), np.stack(halves(inner)), turns


def split(x):
    high = x.astype(BF16)
    return high, (x - high.astype(F32)).astype(BF16)


def dot(a, b):
    return jnp.dot(a, b, preferred_element_type=F32)


def dot_nt(a, b):
    return lax.dot_general(a, b, (((1,), (1,)), ((), ())), preferred_element_type=F32)


def dot3(a, b):
    return dot(a[0], b[0]) + dot(a[0], b[1]) + dot(a[1], b[0])


def dot3_wide(a, b):
    columns = b[0].shape[1]
    both = dot(a[0], jnp.concatenate(b, 1))
    return both[:, :columns] + both[:, columns:] + dot(a[1], b[0])


def product(a, b):
    return a[0] * b[0] - a[1] * b[1], a[0] * b[1] + a[1] * b[0]


def conj(a):
    return a[0], -a[1]


def kernel(
    n_ch,
    q_hbm, k_hbm, v_hbm, ct_hbm, basis_hbm, weight_hbm, rate_hbm, skip_hbm, gain_hbm,
    outer_hbm, back_hbm, inner_hbm, turns_hbm,
    out_ref, gq_ref, gk_ref, gv_ref, gf_ref,
    q_ref, k_ref, v_ref, ct_ref, basis_ref, weight_ref, rate_ref, skip_ref, gain_ref,
    outer_ref, back_ref, inner_ref, turns,
    send_kg, send_c, send_m, send_y, send_s, send_f,
    recv_kg, recv_c, recv_m, recv_y, recv_s, recv_f,
    all_basis, rates, wide_basis, own_grad,
    load_sem, send_sem, recv_sem,
):
    width, rows = send_c.shape
    features = basis_ref.shape[0]
    each = features // N_CTX
    group = width // N_CTX
    full_width = width * n_ch
    me = lax.axis_index("ctx")
    my_ch = lax.axis_index("ch")
    my_y, my_z, my_core = me // (N_Z * N_CORE), me // N_CORE % N_Z, me % N_CORE
    y_mate = (my_y + 1) % N_Y * N_Z * N_CORE + me % (N_Z * N_CORE)
    core_mate = me - my_core + (my_core + 1) % N_CORE

    peers = []
    for dy in (1, 0):
        for dc in (1, 0):
            corner = lax.rem(my_y + dy, N_Y) * (N_Z * N_CORE) + lax.rem(my_core + dc, N_CORE)
            for dz in (4, 3, 5, 2, 6, 1, 7, 0):
                if (dy, dz, dc) != (0, 0, 0):
                    peers.append(corner + lax.rem(my_z + dz, N_Z) * N_CORE)
    half = N_CTX // 2
    other_y = lax.rem(my_y + 1, N_Y)
    far_first = sorted(
        ((dy, dx) for dy in range(N_CH_Y) for dx in range(N_CH_X) if (dy, dx) != (0, 0)),
        key=lambda d: -2 * min(d[0], N_CH_Y - d[0]) - min(d[1], N_CH_X - d[1]),
    )
    ch_peers = [
        lax.rem(my_ch // N_CH_X + dy, N_CH_Y) * N_CH_X + lax.rem(my_ch % N_CH_X + dx, N_CH_X)
        for dy, dx in far_first
    ]

    barrier = pltpu.get_barrier_semaphore()

    for to in peers:
        pl.semaphore_signal(barrier, inc=1, device_id={"ctx": to}, device_id_type=MESH)
    for to in ch_peers:
        pl.semaphore_signal(barrier, inc=1, device_id={"ch": to}, device_id_type=MESH)

    sources = (
        k_hbm, v_hbm, basis_hbm, weight_hbm, rate_hbm,
        q_hbm, ct_hbm, skip_hbm, gain_hbm, outer_hbm, back_hbm, inner_hbm, turns_hbm,
    )
    targets = (
        k_ref, v_ref, basis_ref, weight_ref, rate_ref,
        q_ref, ct_ref, skip_ref, gain_ref, outer_ref, back_ref, inner_ref, turns,
    )
    loads = [
        pltpu.make_async_copy(source, target, load_sem.at[at])
        for at, (source, target) in enumerate(zip(sources, targets))
    ]
    for load in loads:
        load.start()

    def exchange(slot, src, dst, to_peers):
        mine = pl.ds(pl.multiple_of(me * group, group), group)
        for to in to_peers:
            pltpu.make_async_remote_copy(
                src_ref=src.at[pl.ds(pl.multiple_of(to * group, group), group)],
                dst_ref=dst.at[mine],
                send_sem=send_sem.at[slot],
                recv_sem=recv_sem.at[slot],
                device_id={"ctx": to},
                device_id_type=MESH,
            ).start()

    def planes_in_order(y, act):
        for z in range(N_Z):
            for core in (lax.rem(my_core + 1, N_CORE), my_core):
                to = (y * N_Z + z) * N_CORE + core

                @pl.when(to != me)
                def _():
                    act(to)

    def give_back(slot, src, dst, to):
        exchange(slot, src, dst, [to])

    def keep_own(src, dst):
        mine = pl.ds(pl.multiple_of(me * group, group), group)
        dst[mine] = src[mine]

    def wait_for(slot, ref, extent, axis, to):
        return pltpu.make_async_remote_copy(
            src_ref=ref.at[extent],
            dst_ref=ref.at[extent],
            send_sem=send_sem.at[slot],
            recv_sem=recv_sem.at[slot],
            device_id={axis: to},
            device_id_type=MESH,
        )

    def blocks_wait(slot, ref):
        return wait_for(slot, ref, pl.ds(0, (N_CTX - 1) * group), "ctx", core_mate)

    def turned(real, imag):
        cos_w, sin_w = turns[0], turns[1]
        return jnp.concatenate([real * cos_w - imag * sin_w, real * sin_w + imag * cos_w], 1)

    def forward(block):
        first = dot3_wide((outer_ref[0], outer_ref[1]), split(block))
        parts = turned(first[:width], first[width:])
        spectrum = dot3(split(parts), (inner_ref[0], inner_ref[1]))
        return spectrum[:, :rows], spectrum[:, rows:]

    def inverse(conjugates):
        stacked = jnp.concatenate([jnp.concatenate(pair, 1) for pair in conjugates], 0)
        first = dot3(split(stacked), (inner_ref[0], inner_ref[1]))
        columns = []
        for at in range(len(conjugates)):
            part = first[at * width : (at + 1) * width]
            z = turned(part[:, :rows], part[:, rows:])
            columns.append(jnp.concatenate([z[:, :rows], -z[:, rows:]], 0))
        return split(jnp.concatenate(columns, 1))

    side = width // N_Y

    def blocks_of(y, columns, multiply):
        take = pl.ds(pl.multiple_of(y * side, side), side)
        return take, multiply((back_ref[0, take], back_ref[1, take]), columns)

    for load in loads[:5]:
        load.wait()
    rate = jnp.broadcast_to(rate_ref[...], (rows, width)).T
    rates[...] = rate
    lane = lax.broadcasted_iota(jnp.int32, (width, rows), 1)
    decay = jnp.exp(-rate * (me * rows + lane).astype(F32))
    weight = weight_ref[...].astype(F32).T.astype(BF16)
    filter_block = dot(weight, basis_ref[...]) * decay
    send_kg[:, :group] = filter_block.reshape(N_CTX, group, rows)
    keys = k_ref[...].astype(F32)
    values = v_ref[...].astype(F32)
    gated = (keys * values).T
    send_kg[:, group:] = gated.reshape(N_CTX, group, rows)
    all_basis[me] = basis_ref[...].astype(F32)

    pl.semaphore_wait(barrier, N_CTX + n_ch - 2)
    for to in peers:
        pltpu.make_async_remote_copy(
            src_ref=send_kg.at[to],
            dst_ref=recv_kg.at[me],
            send_sem=send_sem.at[0],
            recv_sem=recv_sem.at[0],
            device_id={"ctx": to},
            device_id_type=MESH,
        ).start()
    recv_kg[me] = send_kg[me]

    def pass_on(slot, origin, away):
        at = me + (lax.rem(my_z + origin, N_Z) - my_z) * N_CORE
        to = me + (lax.rem(my_z + away, N_Z) - my_z) * N_CORE
        pltpu.make_async_remote_copy(
            src_ref=all_basis.at[at],
            dst_ref=all_basis.at[at],
            send_sem=send_sem.at[slot],
            recv_sem=recv_sem.at[slot],
            device_id={"ctx": to},
            device_id_type=MESH,
        ).start()

    for away in (2, N_Z - 2, 1, N_Z - 1):
        pass_on(4, 0, away)

    for load in loads[5:]:
        load.wait()
    queries = q_ref[...].astype(F32).T
    scaled = (ct_ref[...].astype(F32) * gain_ref[...]).T
    skip = jnp.broadcast_to(skip_ref[...], (rows, width)).T
    gain = gain_ref[...]

    first_wait = wait_for(0, recv_kg, pl.ds(0, N_CTX - 1), "ctx", core_mate)
    first_wait.wait_recv()
    arrivals = [recv_kg[:, at : at + group].reshape(width, rows) for at in (0, group)]
    both_first = dot3((outer_ref[0], outer_ref[1]), split(jnp.concatenate(arrivals, 1)))
    turned_both = [
        turned(both_first[:width, at : at + rows], both_first[width:, at : at + rows])
        for at in (0, rows)
    ]
    spectra = dot3(split(jnp.concatenate(turned_both, 0)), (inner_ref[0], inner_ref[1]))
    kernel_spec = spectra[:width, :rows], spectra[:width, rows:]
    gated_spec = spectra[width:, :rows], spectra[width:, rows:]
    columns = inverse([conj(product(gated_spec, kernel_spec))])
    for y, some in ((other_y, peers[:half]), (my_y, peers[half:])):
        take, blocks = blocks_of(y, columns, dot3_wide)
        send_c[take] = blocks
        exchange(2, send_c, recv_c, some)
    keep_own(send_c, recv_c)

    wait_for(4, all_basis, pl.ds(0, 4), "ctx", core_mate).wait_recv()
    pass_on(10, N_Z - 2, 2)
    pass_on(10, N_Z - 2, 1)
    pass_on(10, 2, N_Z - 1)

    own_rate = rates[pl.ds(pl.multiple_of(me * group, group), group)]
    row = lax.broadcasted_iota(jnp.int32, (width, rows), 0)
    own_decay = jnp.exp(
        -jnp.concatenate([own_rate] * N_CTX, 0) * (row // group * rows + lane).astype(F32)
    )

    blocks_wait(2, recv_c).wait_recv()
    mixed = recv_c[...] + skip * gated
    signal = queries * mixed
    send_s[0:1] = jnp.sum(signal * signal, axis=0, keepdims=True)
    send_s[1:2] = jnp.sum(signal * scaled, axis=0, keepdims=True)

    for to in ch_peers:
        pltpu.make_async_remote_copy(
            src_ref=send_s,
            dst_ref=recv_s.at[my_ch],
            send_sem=send_sem.at[3],
            recv_sem=recv_sem.at[3],
            device_id={"ch": to},
            device_id_type=MESH,
        ).start()

    recv_s[my_ch] = send_s[...]

    wait_for(10, all_basis, pl.ds(0, 3), "ctx", core_mate).wait_recv()
    for z in range(N_Z):
        slot = my_y * N_Z * N_CORE + z * N_CORE + my_core
        pltpu.make_async_remote_copy(
            src_ref=all_basis.at[slot],
            dst_ref=all_basis.at[slot],
            send_sem=send_sem.at[8],
            recv_sem=recv_sem.at[8],
            device_id={"ctx": y_mate},
            device_id_type=MESH,
        ).start()

    sums_wait = wait_for(3, recv_s, pl.ds(0, n_ch - 1), "ch", lax.rem(my_ch + 1, n_ch))
    sums_wait.wait_recv()
    sums = jnp.sum(recv_s[...], axis=0)
    inv_rms = lax.rsqrt(sums[0:1] / full_width + 1e-06)
    pull = inv_rms * inv_rms * inv_rms * sums[1:2] / full_width
    grad_signal = inv_rms * scaled - signal * pull
    grad_mixed = grad_signal * queries
    send_m[...] = grad_mixed
    exchange(5, send_m, recv_m, peers)
    keep_own(send_m, recv_m)

    out_ref[...] = ((signal * inv_rms).T * gain).astype(BF16)
    gq_ref[...] = (grad_signal * mixed).T.astype(BF16)

    wait_for(8, all_basis, pl.ds(0, N_Z), "ctx", y_mate).wait_recv()
    for at in range(N_Y * N_Z):
        slot = at * N_CORE + my_core
        pltpu.make_async_remote_copy(
            src_ref=all_basis.at[slot],
            dst_ref=all_basis.at[slot],
            send_sem=send_sem.at[9],
            recv_sem=recv_sem.at[9],
            device_id={"ctx": core_mate},
            device_id_type=MESH,
        ).start()

    wait_for(9, all_basis, pl.ds(0, N_Y * N_Z), "ctx", core_mate).wait_recv()
    for at in range(N_CTX):
        wide_basis[:, at * rows : (at + 1) * rows] = all_basis[at].astype(BF16)

    blocks_wait(5, recv_m).wait_recv()
    grad_spec = conj(forward(recv_m[...]))
    columns = inverse([product(kernel_spec, grad_spec), product(gated_spec, grad_spec)])
    for y in (other_y, my_y):
        take, blocks = blocks_of(y, columns, dot3)
        send_y[take] = blocks[:, :rows]
        planes_in_order(y, functools.partial(give_back, 6, send_y, recv_y))
        own_grad[take] = blocks[:, rows:]
    keep_own(send_y, recv_y)

    high, low = (part.astype(F32) for part in split(own_grad[...] * own_decay))
    pairs = [
        jnp.concatenate([part[at * group : (at + 1) * group] for part in (high, low)], 0)
        for at in range(N_CTX)
    ]
    total = dot_nt(wide_basis[...], jnp.concatenate(pairs, 1).astype(BF16))
    total = total[:, :group] + total[:, group:]
    own_filter = jnp.concatenate([total, jnp.zeros((features, rows - group), F32)], 1)
    own_filter = pltpu.roll(own_filter, me * group % rows, 1)
    for at in range(N_CTX):
        send_f[at] = own_filter[at * each : (at + 1) * each]

    def give_filter(to):
        pltpu.make_async_remote_copy(
            src_ref=send_f.at[to],
            dst_ref=recv_f.at[me],
            send_sem=send_sem.at[7],
            recv_sem=recv_sem.at[7],
            device_id={"ctx": to},
            device_id_type=MESH,
        ).start()

    for y in (other_y, my_y):
        planes_in_order(y, give_filter)
    recv_f[me] = send_f[me]

    blocks_wait(6, recv_y).wait_recv()
    grad_gated = (recv_y[...] + skip * grad_mixed).T
    gk_ref[...] = (grad_gated * values).astype(BF16)
    gv_ref[...] = (grad_gated * keys).astype(BF16)

    filter_wait = wait_for(7, recv_f, pl.ds(0, N_CTX - 1), "ctx", core_mate)
    filter_wait.wait_recv()
    per = rows // group
    for at in range(width // rows):
        gf_ref[:, at * rows : (at + 1) * rows] = jnp.sum(recv_f[at * per : (at + 1) * per], axis=0)

    first_wait.wait_send()
    blocks_wait(2, send_c).wait_send()
    blocks_wait(5, send_m).wait_send()
    blocks_wait(6, send_y).wait_send()
    sums_wait.wait_send()
    filter_wait.wait_send()
    wait_for(4, all_basis, pl.ds(0, 4), "ctx", core_mate).wait_send()
    wait_for(10, all_basis, pl.ds(0, 3), "ctx", core_mate).wait_send()
    wait_for(8, all_basis, pl.ds(0, N_Z), "ctx", y_mate).wait_send()
    wait_for(9, all_basis, pl.ds(0, N_Y * N_Z), "ctx", core_mate).wait_send()


def store(*refs):
    count = len(refs) // 2
    copies = [
        pltpu.make_async_copy(refs[at], refs[count + at], refs[-1].at[at]) for at in range(count)
    ]
    for copy in copies:
        copy.start()
    for copy in copies:
        copy.wait()


def solution(mesh):
    n_ctx, n_ch = mesh.shape["ctx"], mesh.shape["ch"]
    assert n_ctx == N_CTX and n_ch == N_CH_Y * N_CH_X

    def shards(query, key, value, cotangent, basis, weight, rate, skip, gain):
        rows, width = query.shape
        features = basis.shape[1]
        each = features // n_ctx
        tables = transform_tables(n_ctx, rows, width // n_ctx)
        operands = (
            query, key, value, cotangent, basis.T, weight,
            rate[None, :], skip[None, :], gain[None, :],
            *(jnp.asarray(table) for table in tables),
        )
        inside = pl.BlockSpec(memory_space=pltpu.VMEM)
        outside = pl.BlockSpec(memory_space=pltpu.HBM)
        wide = jax.ShapeDtypeStruct((rows, width), BF16)
        results = (wide, wide, wide, wide, jax.ShapeDtypeStruct((each, width), F32))
        slots = [pltpu.VMEM((n_ctx, 2 * width // n_ctx, rows), F32)]
        slots += [pltpu.VMEM((width, rows), F32)] * 3
        last = [pltpu.VMEM((n_ctx, each, rows), F32)]
        computed = pl.pallas_call(
            functools.partial(kernel, n_ch),
            out_shape=results,
            in_specs=[outside] * len(operands),
            out_specs=(inside,) * 5,
            scratch_shapes=[
                *(pltpu.VMEM(operand.shape, operand.dtype) for operand in operands),
                *slots,
                pltpu.VMEM((2, rows), F32),
                *last,
                *slots,
                pltpu.VMEM((n_ch, 2, rows), F32),
                *last,
                pltpu.VMEM((n_ctx, features, rows), F32),
                pltpu.VMEM((width, rows), F32),
                pltpu.VMEM((features, n_ctx * rows), BF16),
                pltpu.VMEM((width, rows), F32),
                pltpu.SemaphoreType.DMA((len(operands),)),
                pltpu.SemaphoreType.DMA((11,)),
                pltpu.SemaphoreType.DMA((11,)),
            ],
            compiler_params=pltpu.CompilerParams(
                collective_id=0, has_side_effects=True, vmem_limit_bytes=60 * 1024 * 1024
            ),
        )(*operands)
        return pl.pallas_call(
            store,
            out_shape=results,
            in_specs=[inside] * 5,
            out_specs=(outside,) * 5,
            scratch_shapes=[pltpu.SemaphoreType.DMA((5,))],
        )(*computed)

    return jax.shard_map(
        shards,
        mesh=mesh,
        in_specs=(
            P("ctx", "ch"), P("ctx", "ch"), P("ctx", "ch"), P("ctx", "ch"),
            P("ctx", None), P(None, "ch"), P("ch"), P("ch"), P("ch"),
        ),
        out_specs=(P("ctx", "ch"),) * 5,
        check_vma=False,
    )
```
